512 devices in a mesh: wide: 128 (over y, x, z_lo), sub: 4 (over z_hi, core).
Axes of the slice: x: 4, y: 4, z: 16 (z_hi: 2, z_lo: 8; z = z_hi * 8 + z_lo), core: 2. Of those that a mesh axis runs over, the one named last changes fastest.
Arguments:
- spectrum: float32 [1152, 65536], P(None, ('wide', 'sub')), may hold values from 0.1 to 2
- wind_speed: float32 [65536], P(('wide', 'sub')), may hold values from 5 to 40
- wind_dir: float32 [65536], P(('wide', 'sub')), may hold values from -3.140625 to 3.140625
- wet_mask: int32 [512, 128], P('sub'), may hold values 0 or 1
- row_block: int32 [4, 128], P('sub'), may hold values from 0 to 127, each once within a row
- plus_index: int32 [1152], replicated, may hold values from 0 to 1151, as said below
- minus_index: int32 [1152], replicated, may hold values from 0 to 1151, as said below
Outputs:
- final_spectrum: float32 [1152, 65536], P(None, ('wide', 'sub'))
The draws below stay inside these ranges and needn't reach their ends.
Inputs may be any that keep to these rules, and one draw needn't show every extreme that they name: plus_index[b] names a bin 1 or 2 frequencies higher, direction turned 1 to 3 steps up; at the highest frequency it is b itself. minus_index[b] names a bin 1 or 2 frequencies lower, direction turned 1 to 3 steps down; at the lowest frequency it is b itself. Each row of row_block is a permutation.
All inputs are finite; a program needn't handle non-finite values. No bound on the sum of `wet_mask` on one device may be relied on, other than what follows from the above.
Results may differ from the reference program's by a relative error of at most 0.0003.
Values sent between devices are 32-bit elements; how exact they have to be, the bound alone decides.
A program may use at most 128 MiB of HBM per device.

```python
import math
import jax
import jax.numpy as jnp
from jax import lax

ND = 36
NF = 32
NY = 128
STEPS = 2
NB = 1152
BLOCKS = 128
STRIPS = 4
NX = 512
PTS = 65536
N_WIDE = 128
N_SUB = 4


def partner_table(key, sign):
    bin_ids = jnp.arange(NF * ND, dtype=jnp.int32)
    frequency = bin_ids // ND
    direction = bin_ids % ND
    freq_step = jax.random.randint(jax.random.fold_in(key, 1), (NF * ND,), 1, 3)
    turn_step = jax.random.randint(jax.random.fold_in(key, 2), (NF * ND,), 1, 4)
    new_freq = jnp.clip(frequency + sign * freq_step, 0, NF - 1)
    new_dir = jnp.where(new_freq == frequency, direction, (direction + sign * turn_step) % ND)
    return (new_freq * ND + new_dir).astype(jnp.int32)


def draw_plus_index(key, part):
    key = jax.random.fold_in(key, 11)
    return partner_table(key, 1)


def draw_minus_index(key, part):
    key = jax.random.fold_in(key, 12)
    return partner_table(key, -1)


def with_ends(entries, rng, smallest, top_value):
    place = [jax.random.randint(jax.random.fold_in(rng, axis), (), 0, length) for axis, length in enumerate(entries.shape)]
    widest = entries.shape.index(max(entries.shape))
    next_to = place[:widest] + [(place[widest] + 1) % entries.shape[widest]] + place[widest + 1:]
    return entries.at[tuple(place)].set(smallest).at[tuple(next_to)].set(top_value)


def block_levels(stream_key, shape, cuts, low, largest):
    level = 1.0
    for position, blocks in cuts:
        heights = jax.random.uniform(jax.random.fold_in(jax.random.fold_in(stream_key, 6), position), (blocks,), jnp.float32, low / len(cuts), largest / len(cuts))
        level = level * jnp.repeat(jnp.exp(heights), shape[position] // blocks).reshape((-1,) + (1,) * (len(shape) - 1 - position))
    return level


def setup_inputs(seed: int = 0) -> dict:
    key_of = jax.random.split(jax.random.key(seed), 8)
    spectrum = jnp.clip(jnp.exp(math.log(2.0) - 2.9957323 * jax.random.uniform(key_of[0], (NB, PTS), jnp.float32) ** block_levels(key_of[0], (NB, PTS), ((1, 512),), -0.2, 0.2)), 0.1, 2.0)
    wind_speed = jnp.clip(jnp.exp(math.log(40.0) - 2.0794415 * jax.random.uniform(key_of[1], (PTS,), jnp.float32) ** block_levels(key_of[1], (PTS,), ((0, 512),), -0.2, 0.2)), 5.0, 40.0)
    wind_dir = jnp.clip(jax.random.uniform(key_of[2], (PTS,), jnp.float32, -3.140625, 3.140625), -3.140625, 3.140625)
    wet_mask = with_ends((jax.random.randint(key_of[3], (NX, NY), 0, 5) < 4).astype(jnp.int32), jax.random.fold_in(key_of[3], 1), 0, 1)
    row_block = jax.vmap(lambda own: jax.random.permutation(own, BLOCKS))(jax.random.split(key_of[4], STRIPS)).reshape((STRIPS, BLOCKS)).astype(jnp.int32)
    plus_index = draw_plus_index(jax.random.fold_in(key_of[7], 71), 0)
    minus_index = draw_minus_index(jax.random.fold_in(key_of[7], 71), 0)
    return {"spectrum": spectrum, "wind_speed": wind_speed, "wind_dir": wind_dir, "wet_mask": wet_mask, "row_block": row_block, "plus_index": plus_index, "minus_index": minus_index}


WIND_COEF = 0.03
NONLIN_COEF = 0.004
DISS_COEF = 0.02
PLUS_WEIGHT = 0.4096
MINUS_WEIGHT = 3.1605
BOTH_WEIGHT = 1.2945
COURANT_MAX = 0.68

def bin_values(bin_ids):
    frequency = (bin_ids // ND).astype(jnp.float32)
    angles = (bin_ids % ND).astype(jnp.float32) * (2.0 * math.pi / ND)
    bin_rate = 1.0 + 0.1 * frequency
    return (angles, bin_rate, 1.0 / bin_rate)

def inverse_rows(row_block):
    slot_ids = jnp.arange(N_WIDE, dtype=jnp.int32)
    hits = (row_block[:, None, :] == slot_ids[None, :, None]).astype(jnp.int32)
    return lax.optimization_barrier(jnp.sum(hits * slot_ids[None, None, :], axis=2))

def to_grid(stored, inverse):
    layers = stored.shape[0]
    by_slot = stored.reshape(layers, N_WIDE, N_SUB, NY)
    strips = [by_slot[:, :, strip_id][:, inverse[strip_id]] for strip_id in range(N_SUB)]
    return jnp.stack(strips, axis=1).reshape(layers, NX, NY)

def from_grid(grid, row_block):
    layers = grid.shape[0]
    strips = grid.reshape(layers, N_SUB, N_WIDE, NY)
    by_slot = [strips[:, strip_id][:, row_block[strip_id]] for strip_id in range(N_SUB)]
    return jnp.stack(by_slot, axis=2).reshape(layers, N_WIDE * N_SUB * NY)

def local_sources(current, speeds, directions, wet_point, plus_index, minus_index):
    angles, bin_rate, bin_speed = bin_values(jnp.arange(NB, dtype=jnp.int32))
    rounded = current.astype(jnp.bfloat16)
    plus_vals = rounded[plus_index].astype(jnp.float32)
    minus_vals = rounded[minus_index].astype(jnp.float32)
    delta_nl = NONLIN_COEF * bin_rate[:, None] * current * (current * (PLUS_WEIGHT * plus_vals + MINUS_WEIGHT * minus_vals) - 2.0 * BOTH_WEIGHT * plus_vals * minus_vals)
    delta_bf = delta_nl.astype(jnp.bfloat16).astype(jnp.float32)
    returned = jax.ops.segment_sum(delta_bf, plus_index, num_segments=NB) + jax.ops.segment_sum(delta_bf, minus_index, num_segments=NB)
    nonlinear = returned - 2.0 * delta_nl
    phase = 40.0 * bin_speed
    alignment = jnp.cos(angles[:, None] - directions[None, :])
    growth = WIND_COEF * bin_rate[:, None] * jnp.maximum(speeds[None, :] * alignment / phase[:, None] - 1.0, 0.0)
    steepness = jnp.sqrt(lax.optimization_barrier(jnp.mean((bin_rate[:, None] * current) ** 2, axis=0)) + 1e-06)
    damping = DISS_COEF * bin_rate[:, None] * steepness[None, :]
    return wet_point[None, :] * (current + growth * current - damping * current + nonlinear)

def advect(grid, wet_grid):
    angles, bin_rate, bin_speed = bin_values(jnp.arange(NB, dtype=jnp.int32))
    courant_x = (COURANT_MAX * bin_speed * jnp.cos(angles))[:, None, None]
    courant_y = (COURANT_MAX * bin_speed * jnp.sin(angles))[:, None, None]
    padded = jnp.pad(grid, ((0, 0), (1, 1), (1, 1)))
    centre = grid
    upper_row = padded[:, :-2, 1:-1]
    lower_row = padded[:, 2:, 1:-1]
    left_cell = padded[:, 1:-1, :-2]
    right_cell = padded[:, 1:-1, 2:]
    advected = centre - jnp.maximum(courant_x, 0.0) * (centre - upper_row) - jnp.minimum(courant_x, 0.0) * (lower_row - centre) - jnp.maximum(courant_y, 0.0) * (centre - left_cell) - jnp.minimum(courant_y, 0.0) * (right_cell - centre)
    return advected * wet_grid[None]

def reference(spectrum, wind_speed, wind_dir, wet_mask, row_block, plus_index, minus_index):
    slots_all = N_WIDE * N_SUB
    inverse = inverse_rows(row_block)
    wet_grid = wet_mask.astype(jnp.float32)
    wet_points = from_grid(wet_grid[None], row_block)[0]
    speed_rows = wind_speed.reshape(slots_all, NY)
    dir_rows = wind_dir.reshape(slots_all, NY)
    wet_rows = wet_points.reshape(slots_all, NY)
    current = spectrum

    def one_row(pieces):
        return local_sources(pieces[0], pieces[1], pieces[2], pieces[3], plus_index, minus_index)
    for step_index in range(STEPS):
        row_spectra = current.reshape(NB, slots_all, NY).transpose(1, 0, 2)
        sourced = lax.map(one_row, (row_spectra, speed_rows, dir_rows, wet_rows))
        current = sourced.transpose(1, 0, 2).reshape(NB, PTS)
        grid = to_grid(current, inverse)
        grid = advect(grid, wet_grid)
        current = from_grid(grid, row_block)
    return current
```

```python
import functools
import math

import jax
import jax.numpy as jnp
import numpy as np
from jax import lax
from jax.experimental import pallas as pl
from jax.experimental.pallas import tpu as pltpu
from jax.sharding import PartitionSpec as P

ND = 36
NF = 32
NB = ND * NF
NW = 128
NS = 4
TILES = NB // 128
HALF = 5 * 128
SPLIT = 19 * NF

WIND_COEF = 0.03
NONLIN_COEF = 0.004
DISS_COEF = 0.02
PLUS_WEIGHT = 0.4096
MINUS_WEIGHT = 3.1605
BOTH_WEIGHT = 1.2945
COURANT_MAX = 0.68
MESH = pl.DeviceIdType.MESH
F32 = jnp.float32
BF16 = jnp.bfloat16

RATE, GROW_X, GROW_Y, GROW_0, DAMP, DELTA, KEEP, MOVE_X, MOVE_Y, EAST = range(10)


def bin_table():
    new = np.arange(NB)
    k, l = (new % NF).astype(np.float32), (new // NF).astype(np.float32)
    angles = l * np.float32(2.0 * math.pi / ND)
    rate = np.float32(1.0) + np.float32(0.1) * k
    speed = np.float32(1.0) / rate
    cx = np.float32(COURANT_MAX) * speed * np.cos(angles)
    cy = np.float32(COURANT_MAX) * speed * np.sin(angles)
    table = np.zeros((16, NB), np.float32)
    table[RATE] = rate
    table[GROW_X] = WIND_COEF * rate * rate / 40.0 * np.cos(angles)
    table[GROW_Y] = WIND_COEF * rate * rate / 40.0 * np.sin(angles)
    table[GROW_0] = WIND_COEF * rate
    table[DAMP] = DISS_COEF * rate
    table[DELTA] = NONLIN_COEF * rate
    table[KEEP] = 1.0 - np.abs(cx) - np.abs(cy)
    table[MOVE_X] = np.abs(cx)
    table[MOVE_Y] = np.abs(cy)
    table[EAST] = cx > 0
    assert (cy[:SPLIT] >= 0).all() and (cy[SPLIT:] <= 0).all()
    return table


def column_of(w):
    plane, z = w // 8, lax.rem(w, 8)
    y, x = plane // 4, lax.rem(plane, 4)
    turn = lax.rem(y, 2)
    p = y * 4 + x + turn * (3 - 2 * x)
    back = lax.rem(z, 2)
    return z * 16 + p + back * (15 - 2 * p)


def device_of(c):
    z, q = c // 16, lax.rem(c, 16)
    back = lax.rem(z, 2)
    p = q + back * (15 - 2 * q)
    y, i = p // 4, lax.rem(p, 4)
    turn = lax.rem(y, 2)
    x = i + turn * (3 - 2 * i)
    return (y * 4 + x) * 8 + z


def lanes(t, count=1):
    return pl.ds(pl.multiple_of(t * 128, 128), 128 * count)


def build_partners(part_ref, hot_ref):
    rows = lax.broadcasted_iota(jnp.int32, (256, 256), 0)

    def one(t, carry):
        hot_ref[t] = (part_ref[t] == rows).astype(F32).astype(BF16)
        return carry

    lax.fori_loop(0, TILES, one, 0)


def sources(field, wind_x, wind_y, wet, tab_ref, hot_ref, round_ref, pair_ref, delta_ref, add_ref):
    def rounding(t, total):
        f = field[:, lanes(t)]
        round_ref[:, lanes(t)] = f.astype(BF16)
        scaled = f * tab_ref[RATE : RATE + 1, lanes(t)]
        return total + scaled * scaled

    total = lax.fori_loop(0, TILES, rounding, jnp.zeros((128, 128), F32))
    round_ref[:, lanes(TILES)] = round_ref[:, lanes(0)]
    steep = jnp.sqrt(jnp.sum(total, axis=1, keepdims=True) * (1.0 / NB) + 1e-06)
    steep = jnp.broadcast_to(steep, (128, 128))

    def gather(t, carry):
        both = jnp.dot(round_ref[:, lanes(t, 2)], hot_ref[t], preferred_element_type=F32)
        pair_ref[0, :, lanes(t)] = both[:, :128]
        pair_ref[1, :, lanes(lax.rem(t + 1, TILES))] = both[:, 128:]
        return carry

    lax.fori_loop(0, TILES, gather, 0)

    def combine(t, carry):
        f = field[:, lanes(t)]
        plus, minus = pair_ref[0, :, lanes(t)], pair_ref[1, :, lanes(t)]
        row = lambda r: tab_ref[r : r + 1, lanes(t)]
        delta = (row(DELTA) * f) * (
            f * (PLUS_WEIGHT * plus + MINUS_WEIGHT * minus) - (2.0 * BOTH_WEIGHT) * plus * minus
        )
        delta_ref[:, lanes(t)] = delta.astype(BF16)
        growth = jnp.maximum(wind_x * row(GROW_X) + wind_y * row(GROW_Y) - row(GROW_0), 0.0)
        field[:, lanes(t)] = f + growth * f - (row(DAMP) * steep) * f - 2.0 * delta
        return carry

    lax.fori_loop(0, TILES, combine, 0)
    delta_ref[:, lanes(TILES)] = delta_ref[:, lanes(0)]

    def scatter(t, carry):
        back = lax.dot_general(
            delta_ref[:, lanes(t, 2)], hot_ref[t], (((1,), (1,)), ((), ())), preferred_element_type=F32
        )
        add_ref[0, :, lanes(t)] = back[:, :128]
        add_ref[1, :, lanes(lax.rem(t + 1, TILES))] = back[:, 128:]
        return carry

    lax.fori_loop(0, TILES, scatter, 0)

    def finish(t, carry):
        field[:, lanes(t)] = wet * (field[:, lanes(t)] + add_ref[0, :, lanes(t)] + add_ref[1, :, lanes(t)])
        return carry

    lax.fori_loop(0, TILES, finish, 0)


def spread(row):
    return jnp.transpose(jnp.broadcast_to(row, (128, 128)))


def advect(src, dst, west, east, edges, shift, rows, wet, tab_ref):
    lane = lax.broadcasted_iota(jnp.int32, (128, 128), 1)
    top, bottom = rows == 0.0, rows == float(NW - 1)
    for t in range(TILES):
        at = slice(t * 128, t * 128 + 128)
        f = src[:, at]
        high = f.astype(BF16)
        low = (f - high.astype(F32)).astype(BF16)
        moved = jnp.dot(shift, jnp.concatenate([high, low], axis=0), preferred_element_type=F32)
        above = jnp.where(top, edges[0:1, at], moved[:128])
        below = jnp.where(bottom, edges[8:9, at], moved[128:])
        row = lambda r: tab_ref[r : r + 1, at]
        near_x = jnp.where(row(EAST) > 0.5, above, below)
        if t < 4:
            near_y = west[:, at]
        elif t > 4:
            near_y = east[:, (t - 4) * 128 : (t - 3) * 128]
        else:
            near_y = jnp.where(lane < SPLIT - 512, west[:, at], east[:, 0:128])
        dst[:, at] = wet * (row(KEEP) * f + row(MOVE_X) * near_x + row(MOVE_Y) * near_y)


def kernel(
    spectrum,
    speed,
    direction,
    wet_ref,
    order_ref,
    part_ref,
    tab_ref,
    out,
    first,
    second,
    last,
    wind_out,
    wind_in,
    west,
    east,
    edge_out,
    edge_in,
    hot,
    rounded,
    pair,
    delta,
    add,
    send_a,
    recv_a,
    send_w,
    recv_w,
    send_h,
    recv_h,
    send_e,
    recv_e,
    send_b,
    recv_b,
    spare,
    spare_w,
):
    me = lax.axis_index("wide")
    strip = lax.axis_index("sub")
    column = column_of(me)
    lower, upper = column > 0, column < NW - 1
    to_lower, to_upper = device_of(jnp.maximum(column - 1, 0)), device_of(jnp.minimum(column + 1, NW - 1))
    has_above, has_below = strip > 0, strip < NS - 1

    for k in range(2):
        for is_there, blank in (
            (lower, west.at[k]),
            (upper, east.at[k]),
            (has_above, edge_in.at[k, 0:8]),
            (has_below, edge_in.at[k, 8:16]),
        ):

            @pl.when(jnp.logical_not(is_there))
            def _(blank=blank):
                blank[...] = jnp.zeros(blank.shape, F32)

    barrier = pltpu.get_barrier_semaphore()

    def greet(i, carry):
        pl.semaphore_signal(
            barrier, inc=1, device_id={"wide": lax.rem(me + i, NW)}, device_id_type=MESH
        )
        return carry

    lax.fori_loop(1, NW, greet, 0)

    @pl.when(has_above)
    def _():
        pl.semaphore_signal(barrier, inc=1, device_id={"sub": strip - 1}, device_id_type=MESH)

    @pl.when(has_below)
    def _():
        pl.semaphore_signal(barrier, inc=1, device_id={"sub": strip + 1}, device_id_type=MESH)

    row_ids = lax.broadcasted_iota(jnp.int32, (128, 128), 0).astype(F32)
    lane_ids = lax.broadcasted_iota(jnp.int32, (128, 128), 1).astype(F32)
    ones = jnp.ones((128, 128), BF16)
    order = order_ref[...].astype(F32)
    rows = spread(order)
    wet_grid = wet_ref[...].astype(F32)
    mine = jnp.sum(jnp.where(lane_ids == me.astype(F32), order, 0.0), axis=1, keepdims=True)
    own_wet = jnp.where(row_ids == mine, wet_grid, 0.0).astype(BF16)
    own_wet = lax.dot_general(own_wet, ones, (((0,), (0,)), ((), ())), preferred_element_type=F32)
    col_wet = jnp.where(lane_ids == column.astype(F32), wet_grid, 0.0).astype(BF16)
    col_wet = jnp.dot(col_wet, ones, preferred_element_type=F32).astype(BF16)
    pick = (lane_ids == rows).astype(F32).astype(BF16)
    col_wet = jnp.dot(pick, col_wet, preferred_element_type=F32)
    above_hot = (order == rows - 1.0).astype(F32)
    below_hot = (order == rows + 1.0).astype(F32)
    shift = jnp.concatenate([above_hot, below_hot], axis=0)
    shift = jnp.concatenate([shift, shift], axis=1).astype(BF16)

    wind_x = spread(speed[...] * jnp.cos(direction[...]))
    wind_y = spread(speed[...] * jnp.sin(direction[...]))
    wind_out[...] = jnp.where(lane_ids < 64.0, wind_x, wind_y)

    build_partners(part_ref, hot)
    for t in range(TILES):
        block = jnp.concatenate([spectrum[pl.ds(4 * t + i, NF, stride=ND), :] for i in range(4)], axis=0)
        first[:, t * 128 : t * 128 + 128] = jnp.transpose(block)
    sources(first, wind_x, wind_y, own_wet, tab_ref, hot, rounded, pair, delta, add)

    pl.semaphore_wait(barrier, NW - 1 + has_above.astype(jnp.int32) + has_below.astype(jnp.int32))

    one = lambda ref, i: ref.at[pl.ds(i, 1)]
    pltpu.make_async_copy(one(first, column), one(second, me), recv_a).start()
    pltpu.make_async_copy(one(first, column), one(spare, 0), send_a).start()
    pltpu.make_async_copy(one(wind_out, column), one(wind_in, me), recv_w).start()
    pltpu.make_async_copy(one(wind_out, column), one(spare_w, 0), send_w).start()

    def send_out(i, carry):
        w = lax.rem(me + i, NW)
        c = column_of(w)
        for src, dst, s, r in ((wind_out, wind_in, send_w, recv_w), (first, second, send_a, recv_a)):
            pltpu.make_async_remote_copy(
                one(src, c), one(dst, me), s, r, device_id={"wide": w}, device_id_type=MESH
            ).start()
        return carry

    lax.fori_loop(1, NW, send_out, 0)

    def wait_rows(ref, sem):
        pltpu.make_async_copy(ref, ref, sem).wait()

    def halo(k, field):
        total_top = jnp.zeros((1, 128), F32)
        for t in range(TILES):
            at = slice(t * 128, t * 128 + 128)
            f = field[:, at]
            edge_out[k, 0:1, at] = jnp.sum(jnp.where(rows == float(NW - 1), f, 0.0), axis=0, keepdims=True)
            edge_out[k, 8:9, at] = jnp.sum(jnp.where(rows == 0.0, f, 0.0), axis=0, keepdims=True)
        copies = (
            (upper, lower, field.at[:, 0:HALF], west.at[k], {"wide": to_upper}, send_h.at[k, 0], recv_h.at[k, 0]),
            (lower, upper, field.at[:, NB - HALF : NB], east.at[k], {"wide": to_lower}, send_h.at[k, 1], recv_h.at[k, 1]),
            (
                has_below,
                has_above,
                edge_out.at[k, 0:8],
                edge_in.at[k, 0:8],
                {"sub": jnp.minimum(strip + 1, NS - 1)},
                send_e.at[k, 0],
                recv_e.at[k, 0],
            ),
            (
                has_above,
                has_below,
                edge_out.at[k, 8:16],
                edge_in.at[k, 8:16],
                {"sub": jnp.maximum(strip - 1, 0)},
                send_e.at[k, 1],
                recv_e.at[k, 1],
            ),
        )
        for sends, gets, src, dst, to, s, r in copies:
            copy = pltpu.make_async_remote_copy(src, dst, s, r, device_id=to, device_id_type=MESH)
            pl.when(sends)(copy.start)
        for sends, gets, src, dst, to, s, r in copies:
            copy = pltpu.make_async_remote_copy(src, dst, s, r, device_id=to, device_id_type=MESH)
            pl.when(gets)(copy.wait_recv)
            pl.when(sends)(copy.wait_send)

    wait_rows(second, recv_a)
    halo(0, second)
    wait_rows(first, send_a)
    advect(second, first, west.at[0], east.at[0], edge_in.at[0], shift, rows, col_wet, tab_ref)

    wait_rows(wind_in, recv_w)
    both = wind_in[...]
    turned = pltpu.roll(both, 64, 1)
    wind_x = jnp.where(lane_ids < 64.0, both, turned)
    wind_y = jnp.where(lane_ids < 64.0, turned, both)
    sources(first, wind_x, wind_y, col_wet, tab_ref, hot, rounded, pair, delta, add)
    halo(1, first)
    advect(first, second, west.at[1], east.at[1], edge_in.at[1], shift, rows, col_wet, tab_ref)

    pltpu.make_async_copy(one(second, me), one(last, column), recv_b).start()
    pltpu.make_async_copy(one(second, me), one(spare, 8), send_b).start()

    def send_back(i, carry):
        w = lax.rem(me + i, NW)
        pltpu.make_async_remote_copy(
            one(second, w), one(last, column), send_b, recv_b, device_id={"wide": w}, device_id_type=MESH
        ).start()
        return carry

    lax.fori_loop(1, NW, send_back, 0)
    wait_rows(last, recv_b)
    for t in range(TILES):
        block = jnp.transpose(last[:, t * 128 : t * 128 + 128])
        for i in range(4):
            out[pl.ds(4 * t + i, NF, stride=ND), :] = block[i * NF : (i + 1) * NF]
    wait_rows(wind_out, send_w)
    wait_rows(second, send_b)


def local(spectrum, wind_speed, wind_dir, wet_mask, row_block, plus_index, minus_index):
    new = np.arange(NB)
    old = jnp.asarray((new % NF) * ND + new // NF)
    turned = lambda index: lax.rem(index, ND) * NF + lax.div(index, ND)
    up, down = turned(plus_index)[old], turned(minus_index)[old]
    up = up.reshape(TILES, 1, 128)
    down = jnp.roll(down.reshape(TILES, 1, 128), -1, axis=0)
    base = jnp.arange(TILES, dtype=jnp.int32).reshape(TILES, 1, 1) * 128
    part = lax.rem(jnp.concatenate([up, down], axis=2) - base + NB, NB)
    dma, f32 = pltpu.SemaphoreType.DMA, F32
    vmem = pl.BlockSpec(memory_space=pltpu.VMEM)
    wide = NB + 128
    return pl.pallas_call(
        kernel,
        out_shape=jax.ShapeDtypeStruct((NB, 128), f32),
        in_specs=[vmem] * 7,
        out_specs=vmem,
        scratch_shapes=[
            pltpu.VMEM((128, NB), f32),
            pltpu.VMEM((128, NB), f32),
            pltpu.VMEM((128, NB), f32),
            pltpu.VMEM((128, 128), f32),
            pltpu.VMEM((128, 128), f32),
            pltpu.VMEM((2, 128, HALF), f32),
            pltpu.VMEM((2, 128, HALF), f32),
            pltpu.VMEM((2, 16, NB), f32),
            pltpu.VMEM((2, 16, NB), f32),
            pltpu.VMEM((TILES, 256, 256), BF16),
            pltpu.VMEM((128, wide), BF16),
            pltpu.VMEM((2, 128, NB), f32),
            pltpu.VMEM((128, wide), BF16),
            pltpu.VMEM((2, 128, NB), f32),
            dma,
            dma,
            dma,
            dma,
            dma((2, 2)),
            dma((2, 2)),
            dma((2, 2)),
            dma((2, 2)),
            dma,
            dma,
            pltpu.VMEM((16, NB), f32),
            pltpu.VMEM((8, 128), f32),
        ],
        compiler_params=pltpu.CompilerParams(
            collective_id=0, has_side_effects=True, vmem_limit_bytes=48 * 2**20
        ),
    )(
        spectrum,
        wind_speed.reshape(1, 128),
        wind_dir.reshape(1, 128),
        wet_mask,
        row_block,
        part,
        jnp.asarray(bin_table()),
    )


def solution(mesh):
    placed = (
        P(None, ("wide", "sub")),
        P(("wide", "sub")),
        P(("wide", "sub")),
        P("sub", None),
        P("sub", None),
        P(),
        P(),
    )
    return jax.shard_map(
        local, mesh=mesh, in_specs=placed, out_specs=P(None, ("wide", "sub")), check_vma=False
    )
```

```python
import functools
import math

import jax
import jax.numpy as jnp
import numpy as np
from jax import lax
from jax.experimental import pallas as pl
from jax.experimental.pallas import tpu as pltpu
from jax.sharding import PartitionSpec as P

ND = 36
NF = 32
NB = ND * NF
NW = 128
NS = 4
TILES = NB // 128
HALF = 5 * 128
SPLIT = 19 * NF

WIND_COEF = 0.03
NONLIN_COEF = 0.004
DISS_COEF = 0.02
PLUS_WEIGHT = 0.4096
MINUS_WEIGHT = 3.1605
BOTH_WEIGHT = 1.2945
COURANT_MAX = 0.68
MESH = pl.DeviceIdType.MESH
F32 = jnp.float32
BF16 = jnp.bfloat16

RATE, GROW_X, GROW_Y, GROW_0, DAMP, DELTA, KEEP, MOVE_UP, MOVE_DOWN, MOVE_Y = range(10)


def bin_table():
    new = np.arange(NB)
    k, l = (new % NF).astype(np.float32), (new // NF).astype(np.float32)
    angles = l * np.float32(2.0 * math.pi / ND)
    rate = np.float32(1.0) + np.float32(0.1) * k
    speed = np.float32(1.0) / rate
    cx = np.float32(COURANT_MAX) * speed * np.cos(angles)
    cy = np.float32(COURANT_MAX) * speed * np.sin(angles)
    table = np.zeros((16, NB), np.float32)
    table[RATE] = rate
    table[GROW_X] = WIND_COEF * rate * rate / 40.0 * np.cos(angles)
    table[GROW_Y] = WIND_COEF * rate * rate / 40.0 * np.sin(angles)
    table[GROW_0] = WIND_COEF * rate
    table[DAMP] = DISS_COEF * rate
    table[DELTA] = NONLIN_COEF * rate
    table[KEEP] = 1.0 - np.abs(cx) - np.abs(cy)
    table[MOVE_UP] = np.maximum(cx, 0.0)
    table[MOVE_DOWN] = np.maximum(-cx, 0.0)
    table[MOVE_Y] = np.abs(cy)
    assert (cy[:SPLIT] >= 0).all() and (cy[SPLIT:] <= 0).all()
    return table


def column_of(w):
    plane, z = w // 8, lax.rem(w, 8)
    y, x = plane // 4, lax.rem(plane, 4)
    turn = lax.rem(y, 2)
    p = y * 4 + x + turn * (3 - 2 * x)
    back = lax.rem(z, 2)
    return z * 16 + p + back * (15 - 2 * p)


def device_of(c):
    z, q = c // 16, lax.rem(c, 16)
    back = lax.rem(z, 2)
    p = q + back * (15 - 2 * q)
    y, i = p // 4, lax.rem(p, 4)
    turn = lax.rem(y, 2)
    x = i + turn * (3 - 2 * i)
    return (y * 4 + x) * 8 + z


def lanes(t, count=1):
    start = t * 128 if isinstance(t, int) else pl.multiple_of(t * 128, 128)
    return pl.ds(start, 128 * count)


def chunk(g, size=32):
    return pl.ds(pl.multiple_of(g * size, size), size)


def spread(row):
    return jnp.transpose(jnp.broadcast_to(row, (128, 128)))


def build_partners(up_ref, down_ref, column_ref, hot_ref):
    lane = lax.broadcasted_iota(jnp.int32, (128, 128), 1).astype(F32)
    for side, ref in enumerate((up_ref, down_ref)):
        index = ref[...].astype(F32)
        frequency = jnp.floor((index + 0.5) * (1.0 / ND))
        index = (index - ND * frequency) * NF + frequency
        index = jnp.transpose(jnp.concatenate([index, jnp.zeros((128 - TILES, 128), F32)], axis=0))
        for r in range(TILES):
            column_ref[side, r * 128 : r * 128 + 128, :] = jnp.broadcast_to(index[:, r : r + 1], (128, 128))
    for t in range(TILES):
        for side in range(2):
            tile = (t + side) % TILES
            index = [column_ref[side, pl.ds(4 * tile + i, NF, stride=ND), :] for i in range(4)]
            index = jnp.concatenate(index, axis=0) - 128.0 * t
            index = jnp.where(index < 0.0, index + NB, index)
            both = [(index == lane + 128.0 * half).astype(F32).astype(BF16) for half in range(2)]
            hot_ref[t, side * 128 : side * 128 + 128, :] = jnp.concatenate(both, axis=1)


def sources(field, wind_x, wind_y, wet, tab_ref, hot_ref, round_ref, pair_ref, delta_ref, add_ref):
    total = jnp.zeros((128, 128), F32)
    for t in range(TILES):
        f = field[:, lanes(t)]
        round_ref[:, lanes(t)] = f.astype(BF16)
        scaled = f * tab_ref[RATE : RATE + 1, lanes(t)]
        total = total + scaled * scaled
    round_ref[:, lanes(TILES)] = round_ref[:, lanes(0)]
    steep = jnp.sqrt(jnp.sum(total, axis=1, keepdims=True) * (1.0 / NB) + 1e-06)
    steep = jnp.broadcast_to(steep, (128, 128))

    def gather(t):
        both = lax.dot_general(
            round_ref[:, lanes(t, 2)], hot_ref[t], (((1,), (1,)), ((), ())), preferred_element_type=F32
        )
        pair_ref[0, :, lanes(t)] = both[:, :128]
        pair_ref[1, :, lanes((t + 1) % TILES)] = both[:, 128:]

    for t in range(TILES):
        gather(t)

    def combine(t):
        f = field[:, lanes(t)]
        plus, minus = pair_ref[0, :, lanes(t)], pair_ref[1, :, lanes(t)]
        row = lambda r: tab_ref[r : r + 1, lanes(t)]
        delta = (row(DELTA) * f) * (
            f * (PLUS_WEIGHT * plus + MINUS_WEIGHT * minus) - (2.0 * BOTH_WEIGHT) * plus * minus
        )
        delta_ref[:, lanes(t)] = delta.astype(BF16)
        growth = jnp.maximum(wind_x * row(GROW_X) + wind_y * row(GROW_Y) - row(GROW_0), 0.0)
        field[:, lanes(t)] = f + growth * f - (row(DAMP) * steep) * f - 2.0 * delta

    for t in range(TILES):
        combine(t)
    delta_ref[:, lanes(TILES)] = delta_ref[:, lanes(0)]

    def scatter(t):
        back = jnp.dot(delta_ref[:, lanes(t, 2)], hot_ref[t], preferred_element_type=F32)
        add_ref[0, :, lanes(t)] = back[:, :128]
        add_ref[1, :, lanes((t + 1) % TILES)] = back[:, 128:]

    for t in range(TILES):
        scatter(t)

    def finish(t):
        field[:, lanes(t)] = wet * (field[:, lanes(t)] + add_ref[0, :, lanes(t)] + add_ref[1, :, lanes(t)])

    for t in range(TILES):
        finish(t)


def move_rows(src, part, shift, tab_ref):
    for t in range(TILES):
        f = src[:, lanes(t)]
        high = f.astype(BF16)
        low = (f - high.astype(F32)).astype(BF16)
        moved = jnp.dot(shift, jnp.concatenate([high, low], axis=0), preferred_element_type=F32)
        row = lambda r: tab_ref[r : r + 1, lanes(t)]
        part[:, lanes(t)] = row(KEEP) * f + row(MOVE_UP) * moved[:128] + row(MOVE_DOWN) * moved[128:]


def move_columns(g, part, dst, west, east, edges, rows, wet, tab_ref):
    at = chunk(g)
    lane = lax.broadcasted_iota(jnp.int32, (32, 128), 1)
    top, bottom, here = rows[at, :] == 0.0, rows[at, :] == float(NW - 1), wet[at, :]
    for t in range(TILES):
        cols = slice(t * 128, t * 128 + 128)
        row = lambda r: tab_ref[r : r + 1, cols]
        if t < 4:
            near_y = west[at, cols]
        elif t > 4:
            near_y = east[at, (t - 4) * 128 : (t - 3) * 128]
        else:
            near_y = jnp.where(lane < SPLIT - 512, west[at, cols], east[at, 0:128])
        above = jnp.where(top, row(MOVE_UP) * edges[0:1, cols], 0.0)
        below = jnp.where(bottom, row(MOVE_DOWN) * edges[8:9, cols], 0.0)
        dst[at, cols] = here * (part[at, cols] + above + below + row(MOVE_Y) * near_y)


def to_bins(last, out):
    for t in range(TILES):
        block = jnp.transpose(last[:, t * 128 : t * 128 + 128])
        for i in range(4):
            out[pl.ds(4 * t + i, NF, stride=ND), :] = block[i * NF : (i + 1) * NF]


def kernel(
    spectrum_in,
    speed_in,
    direction_in,
    wet_in,
    order_in,
    up_in,
    down_in,
    tab_in,
    last,
    spectrum,
    speed,
    direction,
    wet_ref,
    order_ref,
    up_ref,
    down_ref,
    tab_ref,
    load,
    index_ref,
    first,
    second,
    part,
    wind_row,
    wind_all,
    west,
    east,
    edge_out,
    edge_in,
    rows_ref,
    col_wet_ref,
    hot,
    rounded,
    pair,
    delta,
    add,
    spare,
    spare_w,
    send_a,
    recv_a,
    send_w,
    recv_w,
    send_h,
    recv_h,
    send_e,
    recv_e,
    send_b,
    recv_b,
):
    me = lax.axis_index("wide")
    strip = lax.axis_index("sub")
    plane, z, y = me // 8, lax.rem(me, 8), me // 32
    column = column_of(me)
    lower, upper = column > 0, column < NW - 1
    to_lower, to_upper = device_of(jnp.maximum(column - 1, 0)), device_of(jnp.minimum(column + 1, NW - 1))
    has_above, has_below = strip > 0, strip < NS - 1
    one = lambda ref, i: ref.at[pl.ds(i, 1)]

    for k in range(2):
        for is_there, blank in (
            (lower, west.at[k]),
            (upper, east.at[k]),
            (has_above, edge_in.at[k, 0:8]),
            (has_below, edge_in.at[k, 8:16]),
        ):

            @pl.when(jnp.logical_not(is_there))
            def _(blank=blank):
                blank[...] = jnp.zeros(blank.shape, F32)

    barrier = pltpu.get_barrier_semaphore()
    line_peer = lambda i: plane * 8 + lax.rem(z + i, 8)
    plane_peer = lambda i: lax.rem(plane + i, 16) * 8 + z

    def greet(peer, sem):
        def signal(i, carry):
            pl.semaphore_signal(sem, inc=1, device_id={"wide": peer(i)}, device_id_type=MESH)
            return carry

        return signal

    lax.fori_loop(1, NW, greet(lambda i: lax.rem(me + i, NW), barrier), 0)

    @pl.when(has_above)
    def _():
        pl.semaphore_signal(barrier, inc=1, device_id={"sub": strip - 1}, device_id_type=MESH)

    @pl.when(has_below)
    def _():
        pl.semaphore_signal(barrier, inc=1, device_id={"sub": strip + 1}, device_id_type=MESH)

    inputs = (
        (up_in, up_ref),
        (down_in, down_ref),
        (speed_in, speed),
        (direction_in, direction),
        (wet_in, wet_ref),
        (order_in, order_ref),
        (tab_in, tab_ref),
        (spectrum_in, spectrum),
    )
    inputs = [pltpu.make_async_copy(src, dst, load.at[i]) for i, (src, dst) in enumerate(inputs)]
    for copy in inputs:
        copy.start()
    for copy in inputs[:-1]:
        copy.wait()

    row_ids = lax.broadcasted_iota(jnp.int32, (128, 128), 0).astype(F32)
    lane_ids = lax.broadcasted_iota(jnp.int32, (128, 128), 1).astype(F32)
    ones = jnp.ones((128, 128), BF16)
    order = order_ref[...].astype(F32)
    rows = spread(order)
    rows_ref[...] = rows
    wet_grid = wet_ref[...].astype(F32)
    mine = jnp.sum(jnp.where(lane_ids == me.astype(F32), order, 0.0), axis=1, keepdims=True)
    own_wet = jnp.where(row_ids == mine, wet_grid, 0.0).astype(BF16)
    own_wet = lax.dot_general(own_wet, ones, (((0,), (0,)), ((), ())), preferred_element_type=F32)
    col_wet = jnp.where(lane_ids == column.astype(F32), wet_grid, 0.0).astype(BF16)
    col_wet = jnp.dot(col_wet, ones, preferred_element_type=F32).astype(BF16)
    pick = (lane_ids == rows).astype(F32).astype(BF16)
    col_wet_ref[...] = jnp.dot(pick, col_wet, preferred_element_type=F32)
    above_hot = (order == rows - 1.0).astype(F32)
    below_hot = (order == rows + 1.0).astype(F32)
    shift = jnp.concatenate([above_hot, below_hot], axis=0)
    shift = jnp.concatenate([shift, shift], axis=1).astype(BF16)

    wind_x = speed[...] * jnp.cos(direction[...])
    wind_y = speed[...] * jnp.sin(direction[...])
    wind_row[0:1, 0:128] = wind_x
    wind_row[0:1, 128:256] = wind_y
    build_partners(up_ref, down_ref, index_ref, hot)
    inputs[-1].wait()
    for t in range(TILES):
        block = jnp.concatenate([spectrum[pl.ds(4 * t + i, NF, stride=ND), :] for i in range(4)], axis=0)
        first[:, t * 128 : t * 128 + 128] = jnp.transpose(block)
    sources(first, spread(wind_x), spread(wind_y), own_wet, tab_ref, hot, rounded, pair, delta, add)

    beside = has_above.astype(jnp.int32) + has_below.astype(jnp.int32)
    pl.semaphore_wait(barrier, NW - 1 + beside)

    pltpu.make_async_copy(one(wind_row, 0), one(wind_all, me), recv_w.at[0]).start()
    pltpu.make_async_copy(one(wind_row, 0), one(spare_w, 0), send_w.at[0]).start()

    def send_line(i, carry):
        pltpu.make_async_remote_copy(
            one(wind_row, 0),
            one(wind_all, me),
            send_w.at[0],
            recv_w.at[0],
            device_id={"wide": line_peer(i)},
            device_id_type=MESH,
        ).start()
        return carry

    lax.fori_loop(1, 8, send_line, 0)

    pltpu.make_async_copy(one(first, column), one(second, me), recv_a.at[y]).start()
    pltpu.make_async_copy(one(first, column), one(spare, 0), send_a).start()

    def send_out(i, carry):
        w = lax.rem(me + i, NW)
        pltpu.make_async_remote_copy(
            one(first, column_of(w)),
            one(second, me),
            send_a,
            recv_a.at[y],
            device_id={"wide": w},
            device_id_type=MESH,
        ).start()
        return carry

    lax.fori_loop(1, NW, send_out, 0)

    wind_line = wind_all.at[chunk(plane, 8)]
    pltpu.make_async_copy(wind_line, wind_line, recv_w.at[0]).wait()

    def send_plane(i, carry):
        pltpu.make_async_remote_copy(
            wind_line,
            wind_line,
            send_w.at[1],
            recv_w.at[1],
            device_id={"wide": plane_peer(i)},
            device_id_type=MESH,
        ).start()
        return carry

    lax.fori_loop(1, 16, send_plane, 0)

    def side_copies(k, field):
        def west_copy(g):
            return pltpu.make_async_remote_copy(
                field.at[chunk(g), 0:HALF],
                west.at[k, chunk(g)],
                send_h.at[k, 0, g],
                recv_h.at[k, 0, g],
                device_id={"wide": to_upper},
                device_id_type=MESH,
            )

        def east_copy(g):
            return pltpu.make_async_remote_copy(
                field.at[chunk(g), NB - HALF : NB],
                east.at[k, chunk(g)],
                send_h.at[k, 1, g],
                recv_h.at[k, 1, g],
                device_id={"wide": to_lower},
                device_id_type=MESH,
            )

        return west_copy, east_copy

    def edge_copies(k):
        return [
            (
                sends,
                gets,
                pltpu.make_async_remote_copy(
                    edge_out.at[k, pl.ds(8 * i, 1)],
                    edge_in.at[k, pl.ds(8 * i, 1)],
                    send_e.at[k, i],
                    recv_e.at[k, i],
                    device_id={"sub": to},
                    device_id_type=MESH,
                ),
            )
            for i, sends, gets, to in (
                (0, has_below, has_above, jnp.minimum(strip + 1, NS - 1)),
                (1, has_above, has_below, jnp.maximum(strip - 1, 0)),
            )
        ]

    def start_edges(k, field):
        rows = rows_ref[...]

        for t in range(TILES):
            f = field[:, lanes(t)]
            edge_out[k, 0:1, lanes(t)] = jnp.sum(jnp.where(rows == float(NW - 1), f, 0.0), axis=0, keepdims=True)
            edge_out[k, 8:9, lanes(t)] = jnp.sum(jnp.where(rows == 0.0, f, 0.0), axis=0, keepdims=True)

        for sends, gets, copy in edge_copies(k):
            pl.when(sends)(copy.start)

    def end_edges(k):
        for sends, gets, copy in edge_copies(k):
            pl.when(gets)(copy.wait_recv)
            pl.when(sends)(copy.wait_send)

    west_copy, east_copy = side_copies(0, second)
    west_copy_1, east_copy_1 = side_copies(1, first)

    def pass_on(j, carry):
        g = lax.rem(y + 3 - j, 4)
        pltpu.make_async_copy(second.at[chunk(g)], second.at[chunk(g)], recv_a.at[g]).wait()
        pl.when(upper)(lambda: west_copy(g).start())
        pl.when(lower)(lambda: east_copy(g).start())
        return carry

    lax.fori_loop(0, 4, pass_on, 0)
    start_edges(0, second)
    pltpu.make_async_copy(first, first, send_a).wait()
    move_rows(second, part, shift, tab_ref)
    end_edges(0)

    def first_columns(j, carry):
        g = lax.rem(y + 3 - j, 4)
        pl.when(lower)(lambda: west_copy(g).wait_recv())
        pl.when(upper)(lambda: east_copy(g).wait_recv())
        move_columns(g, part, first, west.at[0], east.at[0], edge_in.at[0], rows_ref, col_wet_ref, tab_ref)
        return carry

    lax.fori_loop(0, 4, first_columns, 0)

    def sent_columns(k):
        west_copy, east_copy = side_copies(k, (second, first)[k])

        def sent(g, carry):
            pl.when(upper)(lambda: west_copy(g).wait_send())
            pl.when(lower)(lambda: east_copy(g).wait_send())
            return carry

        lax.fori_loop(0, 4, sent, 0)

    others = wind_all.at[pl.ds(0, 120)]
    pltpu.make_async_copy(others, others, recv_w.at[1]).wait()
    here = lane_ids == column.astype(F32)
    wind_x, wind_y = (
        jnp.broadcast_to(
            jnp.sum(jnp.where(here, wind_all[:, i * 128 : i * 128 + 128], 0.0), axis=1, keepdims=True), (128, 128)
        )
        for i in range(2)
    )
    sources(first, wind_x, wind_y, col_wet_ref[...], tab_ref, hot, rounded, pair, delta, add)
    start_edges(1, first)
    y_upper, y_lower = to_upper // 32, to_lower // 32

    def start_columns(j, carry):
        pl.when(upper)(lambda: west_copy_1(lax.rem(y_upper + 1 + j, 4)).start())
        pl.when(lower)(lambda: east_copy_1(lax.rem(y_lower + 1 + j, 4)).start())
        return carry

    lax.fori_loop(0, 4, start_columns, 0)
    sent_columns(0)
    move_rows(first, part, shift, tab_ref)
    end_edges(1)

    def last_columns(j, carry):
        g = lax.rem(y + 1 + j, 4)
        pl.when(lower)(lambda: west_copy_1(g).wait_recv())
        pl.when(upper)(lambda: east_copy_1(g).wait_recv())
        move_columns(g, part, second, west.at[1], east.at[1], edge_in.at[1], rows_ref, col_wet_ref, tab_ref)

        def send_back(i, carry):
            w = g * 32 + lax.rem(me + i, 32)
            pltpu.make_async_remote_copy(
                one(second, w), one(last, column), send_b, recv_b, device_id={"wide": w}, device_id_type=MESH
            ).start()
            return carry

        return lax.fori_loop(j // 3, 32, send_back, carry)

    lax.fori_loop(0, 4, last_columns, 0)
    pltpu.make_async_copy(one(second, me), one(last, column), recv_b).start()
    pltpu.make_async_copy(one(second, me), one(spare, 8), send_b).start()
    sent_columns(1)
    pltpu.make_async_copy(wind_all.at[chunk(0, 8)], wind_all.at[chunk(0, 8)], send_w.at[0]).wait()
    pltpu.make_async_copy(others, others, send_w.at[1]).wait()
    pltpu.make_async_copy(last, last, recv_b).wait()
    pltpu.make_async_copy(second, second, send_b).wait()


def local(spectrum, wind_speed, wind_dir, wet_mask, row_block, plus_index, minus_index):
    dma, i32 = pltpu.SemaphoreType.DMA, jnp.int32
    vmem = lambda *shape, dtype=F32: pltpu.VMEM(shape, dtype)
    wide = NB + 128
    received = pl.pallas_call(
        kernel,
        out_shape=jax.ShapeDtypeStruct((128, NB), F32),
        in_specs=[pl.BlockSpec(memory_space=pl.ANY)] * 8,
        out_specs=pl.BlockSpec(memory_space=pltpu.VMEM),
        scratch_shapes=[
            vmem(NB, 128),
            vmem(1, 128),
            vmem(1, 128),
            vmem(128, 128, dtype=i32),
            vmem(1, 128, dtype=i32),
            vmem(TILES, 128, dtype=i32),
            vmem(TILES, 128, dtype=i32),
            vmem(16, NB),
            dma((8,)),
            vmem(2, NB, 128),
            vmem(128, NB),
            vmem(128, NB),
            vmem(128, NB),
            vmem(8, 256),
            vmem(128, 256),
            vmem(2, 128, HALF),
            vmem(2, 128, HALF),
            vmem(2, 16, NB),
            vmem(2, 16, NB),
            vmem(128, 128),
            vmem(128, 128),
            vmem(TILES, 256, 256, dtype=BF16),
            vmem(128, wide, dtype=BF16),
            vmem(2, 128, NB),
            vmem(128, wide, dtype=BF16),
            vmem(2, 128, NB),
            vmem(16, NB),
            vmem(8, 256),
            dma,
            dma((4,)),
            dma((2,)),
            dma((2,)),
            dma((2, 2, 4)),
            dma((2, 2, 4)),
            dma((2, 2)),
            dma((2, 2)),
            dma,
            dma,
        ],
        compiler_params=pltpu.CompilerParams(
            collective_id=0, has_side_effects=True, vmem_limit_bytes=60 * 2**20
        ),
    )(
        spectrum,
        wind_speed.reshape(1, 128),
        wind_dir.reshape(1, 128),
        wet_mask,
        row_block,
        plus_index.reshape(TILES, 128),
        minus_index.reshape(TILES, 128),
        jnp.asarray(bin_table()),
    )
    return pl.pallas_call(to_bins, out_shape=jax.ShapeDtypeStruct((NB, 128), F32))(received)


def solution(mesh):
    placed = (
        P(None, ("wide", "sub")),
        P(("wide", "sub")),
        P(("wide", "sub")),
        P("sub", None),
        P("sub", None),
        P(),
        P(),
    )
    return jax.shard_map(
        local, mesh=mesh, in_specs=placed, out_specs=P(None, ("wide", "sub")), check_vma=False
    )
```

```python
import functools
import math

import jax
import jax.numpy as jnp
import numpy as np
from jax import lax
from jax.experimental import pallas as pl
from jax.experimental.pallas import tpu as pltpu
from jax.sharding import PartitionSpec as P

ND = 36
NF = 32
NB = ND * NF
NW = 128
NS = 4
TILES = NB // 128
HALF = 5 * 128
SPLIT = 19 * NF

WIND_COEF = 0.03
NONLIN_COEF = 0.004
DISS_COEF = 0.02
PLUS_WEIGHT = 0.4096
MINUS_WEIGHT = 3.1605
BOTH_WEIGHT = 1.2945
COURANT_MAX = 0.68
MESH = pl.DeviceIdType.MESH
F32 = jnp.float32
BF16 = jnp.bfloat16

RATE, GROW_X, GROW_Y, GROW_0, DAMP, DELTA, KEEP, MOVE_UP, MOVE_DOWN, MOVE_Y = range(10)


def bin_table():
    new = np.arange(NB)
    k, l = (new % NF).astype(np.float32), (new // NF).astype(np.float32)
    angles = l * np.float32(2.0 * math.pi / ND)
    rate = np.float32(1.0) + np.float32(0.1) * k
    speed = np.float32(1.0) / rate
    cx = np.float32(COURANT_MAX) * speed * np.cos(angles)
    cy = np.float32(COURANT_MAX) * speed * np.sin(angles)
    table = np.zeros((16, NB), np.float32)
    table[RATE] = rate
    table[GROW_X] = WIND_COEF * rate * rate / 40.0 * np.cos(angles)
    table[GROW_Y] = WIND_COEF * rate * rate / 40.0 * np.sin(angles)
    table[GROW_0] = WIND_COEF * rate
    table[DAMP] = DISS_COEF * rate
    table[DELTA] = NONLIN_COEF * rate
    table[KEEP] = 1.0 - np.abs(cx) - np.abs(cy)
    table[MOVE_UP] = np.maximum(cx, 0.0)
    table[MOVE_DOWN] = np.maximum(-cx, 0.0)
    table[MOVE_Y] = np.abs(cy)
    assert (cy[:SPLIT] >= 0).all() and (cy[SPLIT:] <= 0).all()
    return table


def column_of(w, strip):
    w = lax.rem(w + 32 * lax.rem(strip, 2), NW)
    plane, z = w // 8, lax.rem(w, 8)
    z = z + (strip // 2) * (7 - 2 * z)
    y, x = plane // 4, lax.rem(plane, 4)
    turn = lax.rem(y, 2)
    p = y * 4 + x + turn * (3 - 2 * x)
    back = lax.rem(z, 2)
    return z * 16 + p + back * (15 - 2 * p)


def device_of(c, strip):
    z, q = c // 16, lax.rem(c, 16)
    back = lax.rem(z, 2)
    p = q + back * (15 - 2 * q)
    y, i = p // 4, lax.rem(p, 4)
    turn = lax.rem(y, 2)
    x = i + turn * (3 - 2 * i)
    z = z + (strip // 2) * (7 - 2 * z)
    return lax.rem((y * 4 + x) * 8 + z + 96 * lax.rem(strip, 2), NW)


def lanes(t, count=1):
    start = t * 128 if isinstance(t, int) else pl.multiple_of(t * 128, 128)
    return pl.ds(start, 128 * count)


def chunk(g, size=32):
    return pl.ds(pl.multiple_of(g * size, size), size)


def spread(row):
    return jnp.transpose(jnp.broadcast_to(row, (128, 128)))


def build_partners(up_ref, down_ref, column_ref, hot_ref):
    lane = lax.broadcasted_iota(jnp.int32, (128, 128), 1).astype(F32)
    for side, ref in enumerate((up_ref, down_ref)):
        index = ref[...].astype(F32)
        frequency = jnp.floor((index + 0.5) * (1.0 / ND))
        index = (index - ND * frequency) * NF + frequency
        index = jnp.transpose(jnp.concatenate([index, jnp.zeros((128 - TILES, 128), F32)], axis=0))
        for r in range(TILES):
            column_ref[side, r * 128 : r * 128 + 128, :] = jnp.broadcast_to(index[:, r : r + 1], (128, 128))
    for t in range(TILES):
        for side in range(2):
            tile = (t + side) % TILES
            index = [column_ref[side, pl.ds(4 * tile + i, NF, stride=ND), :] for i in range(4)]
            index = jnp.concatenate(index, axis=0) - 128.0 * t
            index = jnp.where(index < 0.0, index + NB, index)
            both = [(index == lane + 128.0 * half).astype(F32).astype(BF16) for half in range(2)]
            hot_ref[t, side * 128 : side * 128 + 128, :] = jnp.concatenate(both, axis=1)


def sources(field, wind_x, wind_y, wet, tab_ref, hot_ref, round_ref, pair_ref, delta_ref, add_ref):
    total = jnp.zeros((128, 128), F32)
    for t in range(TILES):
        f = field[:, lanes(t)]
        round_ref[:, lanes(t)] = f.astype(BF16)
        scaled = f * tab_ref[RATE : RATE + 1, lanes(t)]
        total = total + scaled * scaled
    round_ref[:, lanes(TILES)] = round_ref[:, lanes(0)]
    steep = jnp.sqrt(jnp.sum(total, axis=1, keepdims=True) * (1.0 / NB) + 1e-06)
    steep = jnp.broadcast_to(steep, (128, 128))

    def gather(t):
        both = lax.dot_general(
            round_ref[:, lanes(t, 2)], hot_ref[t], (((1,), (1,)), ((), ())), preferred_element_type=F32
        )
        pair_ref[0, :, lanes(t)] = both[:, :128]
        pair_ref[1, :, lanes((t + 1) % TILES)] = both[:, 128:]

    for t in range(TILES):
        gather(t)

    def combine(t):
        f = field[:, lanes(t)]
        plus, minus = pair_ref[0, :, lanes(t)], pair_ref[1, :, lanes(t)]
        row = lambda r: tab_ref[r : r + 1, lanes(t)]
        delta = (row(DELTA) * f) * (
            f * (PLUS_WEIGHT * plus + MINUS_WEIGHT * minus) - (2.0 * BOTH_WEIGHT) * plus * minus
        )
        delta_ref[:, lanes(t)] = delta.astype(BF16)
        growth = jnp.maximum(wind_x * row(GROW_X) + wind_y * row(GROW_Y) - row(GROW_0), 0.0)
        field[:, lanes(t)] = f + growth * f - (row(DAMP) * steep) * f - 2.0 * delta

    for t in range(TILES):
        combine(t)
    delta_ref[:, lanes(TILES)] = delta_ref[:, lanes(0)]

    def scatter(t):
        back = jnp.dot(delta_ref[:, lanes(t, 2)], hot_ref[t], preferred_element_type=F32)
        add_ref[0, :, lanes(t)] = back[:, :128]
        add_ref[1, :, lanes((t + 1) % TILES)] = back[:, 128:]

    for t in range(TILES):
        scatter(t)

    def finish(t):
        field[:, lanes(t)] = wet * (field[:, lanes(t)] + add_ref[0, :, lanes(t)] + add_ref[1, :, lanes(t)])

    for t in range(TILES):
        finish(t)


def move_rows(src, part, shift, tab_ref):
    for t in range(TILES):
        f = src[:, lanes(t)]
        high = f.astype(BF16)
        low = (f - high.astype(F32)).astype(BF16)
        moved = jnp.dot(shift, jnp.concatenate([high, low], axis=0), preferred_element_type=F32)
        row = lambda r: tab_ref[r : r + 1, lanes(t)]
        part[:, lanes(t)] = row(KEEP) * f + row(MOVE_UP) * moved[:128] + row(MOVE_DOWN) * moved[128:]


def move_columns(g, part, dst, west, east, edges, rows, wet, tab_ref):
    at = chunk(g)
    lane = lax.broadcasted_iota(jnp.int32, (32, 128), 1)
    top, bottom, here = rows[at, :] == 0.0, rows[at, :] == float(NW - 1), wet[at, :]
    for t in range(TILES):
        cols = slice(t * 128, t * 128 + 128)
        row = lambda r: tab_ref[r : r + 1, cols]
        if t < 4:
            near_y = west[at, cols]
        elif t > 4:
            near_y = east[at, (t - 4) * 128 : (t - 3) * 128]
        else:
            near_y = jnp.where(lane < SPLIT - 512, west[at, cols], east[at, 0:128])
        above = jnp.where(top, row(MOVE_UP) * edges[0:1, cols], 0.0)
        below = jnp.where(bottom, row(MOVE_DOWN) * edges[8:9, cols], 0.0)
        dst[at, cols] = here * (part[at, cols] + above + below + row(MOVE_Y) * near_y)


def to_bins(last, out):
    for t in range(TILES):
        block = jnp.transpose(last[:, t * 128 : t * 128 + 128])
        for i in range(4):
            out[pl.ds(4 * t + i, NF, stride=ND), :] = block[i * NF : (i + 1) * NF]


def kernel(
    spectrum_in,
    speed_in,
    direction_in,
    wet_in,
    order_in,
    up_in,
    down_in,
    tab_in,
    last,
    spectrum,
    speed,
    direction,
    wet_ref,
    order_ref,
    up_ref,
    down_ref,
    tab_ref,
    load,
    index_ref,
    first,
    second,
    part,
    wind_row,
    wind_all,
    west,
    east,
    edge_out,
    edge_in,
    rows_ref,
    col_wet_ref,
    hot,
    rounded,
    pair,
    delta,
    add,
    spare,
    spare_w,
    send_a,
    recv_a,
    send_w,
    recv_w,
    send_h,
    recv_h,
    send_e,
    recv_e,
    send_b,
    recv_b,
):
    me = lax.axis_index("wide")
    strip = lax.axis_index("sub")
    plane, z, y = me // 8, lax.rem(me, 8), me // 32
    column = column_of(me, strip)
    lower, upper = column > 0, column < NW - 1
    to_lower, to_upper = device_of(jnp.maximum(column - 1, 0), strip), device_of(jnp.minimum(column + 1, NW - 1), strip)
    to_above = device_of(column, jnp.maximum(strip - 1, 0))
    to_below = device_of(column, jnp.minimum(strip + 1, NS - 1))
    has_above, has_below = strip > 0, strip < NS - 1
    one = lambda ref, i: ref.at[pl.ds(i, 1)]

    for k in range(2):
        for is_there, blank in (
            (lower, west.at[k]),
            (upper, east.at[k]),
            (has_above, edge_in.at[k, 0:8]),
            (has_below, edge_in.at[k, 8:16]),
        ):

            @pl.when(jnp.logical_not(is_there))
            def _(blank=blank):
                blank[...] = jnp.zeros(blank.shape, F32)

    barrier = pltpu.get_barrier_semaphore()
    line_peer = lambda i: plane * 8 + lax.rem(z + i, 8)
    plane_peer = lambda i: lax.rem(plane + i, 16) * 8 + z

    def greet(peer, sem):
        def signal(i, carry):
            pl.semaphore_signal(sem, inc=1, device_id={"wide": peer(i)}, device_id_type=MESH)
            return carry

        return signal

    lax.fori_loop(1, NW, greet(lambda i: lax.rem(me + i, NW), barrier), 0)

    @pl.when(has_above)
    def _():
        pl.semaphore_signal(barrier, inc=1, device_id={"wide": to_above, "sub": strip - 1}, device_id_type=MESH)

    @pl.when(has_below)
    def _():
        pl.semaphore_signal(barrier, inc=1, device_id={"wide": to_below, "sub": strip + 1}, device_id_type=MESH)

    inputs = (
        (up_in, up_ref),
        (down_in, down_ref),
        (speed_in, speed),
        (direction_in, direction),
        (wet_in, wet_ref),
        (order_in, order_ref),
        (tab_in, tab_ref),
        (spectrum_in, spectrum),
    )
    inputs = [pltpu.make_async_copy(src, dst, load.at[i]) for i, (src, dst) in enumerate(inputs)]
    for copy in inputs:
        copy.start()
    for copy in inputs[:-1]:
        copy.wait()

    row_ids = lax.broadcasted_iota(jnp.int32, (128, 128), 0).astype(F32)
    lane_ids = lax.broadcasted_iota(jnp.int32, (128, 128), 1).astype(F32)
    ones = jnp.ones((128, 128), BF16)
    order = order_ref[...].astype(F32)
    rows = spread(order)
    rows_ref[...] = rows
    wet_grid = wet_ref[...].astype(F32)
    mine = jnp.sum(jnp.where(lane_ids == me.astype(F32), order, 0.0), axis=1, keepdims=True)
    own_wet = jnp.where(row_ids == mine, wet_grid, 0.0).astype(BF16)
    own_wet = lax.dot_general(own_wet, ones, (((0,), (0,)), ((), ())), preferred_element_type=F32)
    col_wet = jnp.where(lane_ids == column.astype(F32), wet_grid, 0.0).astype(BF16)
    col_wet = jnp.dot(col_wet, ones, preferred_element_type=F32).astype(BF16)
    pick = (lane_ids == rows).astype(F32).astype(BF16)
    col_wet_ref[...] = jnp.dot(pick, col_wet, preferred_element_type=F32)
    above_hot = (order == rows - 1.0).astype(F32)
    below_hot = (order == rows + 1.0).astype(F32)
    shift = jnp.concatenate([above_hot, below_hot], axis=0)
    shift = jnp.concatenate([shift, shift], axis=1).astype(BF16)

    wind_x = speed[...] * jnp.cos(direction[...])
    wind_y = speed[...] * jnp.sin(direction[...])
    wind_row[0:1, 0:128] = wind_x
    wind_row[0:1, 128:256] = wind_y
    build_partners(up_ref, down_ref, index_ref, hot)
    inputs[-1].wait()
    for t in range(TILES):
        block = jnp.concatenate([spectrum[pl.ds(4 * t + i, NF, stride=ND), :] for i in range(4)], axis=0)
        first[:, t * 128 : t * 128 + 128] = jnp.transpose(block)
    sources(first, spread(wind_x), spread(wind_y), own_wet, tab_ref, hot, rounded, pair, delta, add)

    beside = has_above.astype(jnp.int32) + has_below.astype(jnp.int32)
    pl.semaphore_wait(barrier, NW - 1 + beside)

    pltpu.make_async_copy(one(wind_row, 0), one(wind_all, me), recv_w.at[0]).start()
    pltpu.make_async_copy(one(wind_row, 0), one(spare_w, 0), send_w.at[0]).start()

    def send_line(i, carry):
        pltpu.make_async_remote_copy(
            one(wind_row, 0),
            one(wind_all, me),
            send_w.at[0],
            recv_w.at[0],
            device_id={"wide": line_peer(i)},
            device_id_type=MESH,
        ).start()
        return carry

    lax.fori_loop(1, 8, send_line, 0)

    pltpu.make_async_copy(one(first, column), one(second, me), recv_a.at[plane]).start()
    pltpu.make_async_copy(one(first, column), one(spare, 0), send_a).start()

    def send_out(i, carry):
        w = lax.rem(me + i, NW)
        pltpu.make_async_remote_copy(
            one(first, column_of(w, strip)),
            one(second, me),
            send_a,
            recv_a.at[plane],
            device_id={"wide": w},
            device_id_type=MESH,
        ).start()
        return carry

    lax.fori_loop(1, NW, send_out, 0)

    wind_line = wind_all.at[chunk(plane, 8)]
    pltpu.make_async_copy(wind_line, wind_line, recv_w.at[0]).wait()

    def send_plane(i, carry):
        pltpu.make_async_remote_copy(
            wind_line,
            wind_line,
            send_w.at[1],
            recv_w.at[1],
            device_id={"wide": plane_peer(i)},
            device_id_type=MESH,
        ).start()
        return carry

    lax.fori_loop(1, 16, send_plane, 0)

    def side_copies(k, field):
        def west_copy(g):
            return pltpu.make_async_remote_copy(
                field.at[chunk(g), 0:HALF],
                west.at[k, chunk(g)],
                send_h.at[k, 0, g],
                recv_h.at[k, 0, g],
                device_id={"wide": to_upper},
                device_id_type=MESH,
            )

        def east_copy(g):
            return pltpu.make_async_remote_copy(
                field.at[chunk(g), NB - HALF : NB],
                east.at[k, chunk(g)],
                send_h.at[k, 1, g],
                recv_h.at[k, 1, g],
                device_id={"wide": to_lower},
                device_id_type=MESH,
            )

        return west_copy, east_copy

    def edge_copies(k):
        return [
            (
                sends,
                gets,
                pltpu.make_async_remote_copy(
                    edge_out.at[k, pl.ds(8 * i, 1)],
                    edge_in.at[k, pl.ds(8 * i, 1)],
                    send_e.at[k, i],
                    recv_e.at[k, i],
                    device_id=to,
                    device_id_type=MESH,
                ),
            )
            for i, sends, gets, to in (
                (0, has_below, has_above, {"wide": to_below, "sub": jnp.minimum(strip + 1, NS - 1)}),
                (1, has_above, has_below, {"wide": to_above, "sub": jnp.maximum(strip - 1, 0)}),
            )
        ]

    def start_edges(k, field):
        rows = rows_ref[...]

        for t in range(TILES):
            f = field[:, lanes(t)]
            edge_out[k, 0:1, lanes(t)] = jnp.sum(jnp.where(rows == float(NW - 1), f, 0.0), axis=0, keepdims=True)
            edge_out[k, 8:9, lanes(t)] = jnp.sum(jnp.where(rows == 0.0, f, 0.0), axis=0, keepdims=True)

        for sends, gets, copy in edge_copies(k):
            pl.when(sends)(copy.start)

    def end_edges(k):
        for sends, gets, copy in edge_copies(k):
            pl.when(gets)(copy.wait_recv)
            pl.when(sends)(copy.wait_send)

    west_copy_1, east_copy_1 = side_copies(1, first)

    first_sides = (
        (
            upper,
            lower,
            lambda g: pltpu.make_async_remote_copy(
                second.at[chunk(g, 8), 0:HALF],
                west.at[0, chunk(g, 8)],
                send_h.at[0, 0, 0],
                recv_h.at[0, 0, 0],
                device_id={"wide": to_upper},
                device_id_type=MESH,
            ),
            west.at[0],
        ),
        (
            lower,
            upper,
            lambda g: pltpu.make_async_remote_copy(
                second.at[chunk(g, 8), NB - HALF : NB],
                east.at[0, chunk(g, 8)],
                send_h.at[0, 1, 0],
                recv_h.at[0, 1, 0],
                device_id={"wide": to_lower},
                device_id_type=MESH,
            ),
            east.at[0],
        ),
    )

    def pass_on(j, carry):
        g = lax.rem(plane + 15 - j, 16)
        pltpu.make_async_copy(second.at[chunk(g, 8)], second.at[chunk(g, 8)], recv_a.at[g]).wait()
        for sends, gets, copy, landed in first_sides:
            pl.when(jnp.logical_and(sends, j < 15))(lambda copy=copy: copy(g).start())
        return carry

    lax.fori_loop(0, 16, pass_on, 0)
    start_edges(0, second)
    for sends, gets, copy, landed in first_sides:
        pl.when(sends)(lambda copy=copy: copy(plane).start())
    pltpu.make_async_copy(first, first, send_a).wait()
    move_rows(second, part, shift, tab_ref)
    end_edges(0)

    for i, (sends, gets, copy, landed) in enumerate(first_sides):
        pl.when(gets)(pltpu.make_async_copy(landed, landed, recv_h.at[0, i, 0]).wait)

    def first_columns(g, carry):
        move_columns(g, part, first, west.at[0], east.at[0], edge_in.at[0], rows_ref, col_wet_ref, tab_ref)
        return carry

    lax.fori_loop(0, 4, first_columns, 0)

    def sent_columns(g, carry):
        pl.when(upper)(lambda: west_copy_1(g).wait_send())
        pl.when(lower)(lambda: east_copy_1(g).wait_send())
        return carry

    others = wind_all.at[pl.ds(0, 120)]
    pltpu.make_async_copy(others, others, recv_w.at[1]).wait()
    here = lane_ids == column.astype(F32)
    wind_x, wind_y = (
        jnp.broadcast_to(
            jnp.sum(jnp.where(here, wind_all[:, i * 128 : i * 128 + 128], 0.0), axis=1, keepdims=True), (128, 128)
        )
        for i in range(2)
    )
    sources(first, wind_x, wind_y, col_wet_ref[...], tab_ref, hot, rounded, pair, delta, add)
    start_edges(1, first)
    y_upper, y_lower = to_upper // 32, to_lower // 32

    def start_columns(j, carry):
        pl.when(upper)(lambda: west_copy_1(lax.rem(y_upper + j, 4)).start())
        pl.when(lower)(lambda: east_copy_1(lax.rem(y_lower + j, 4)).start())
        return carry

    lax.fori_loop(0, 4, start_columns, 0)
    for i, (sends, gets, copy, landed) in enumerate(first_sides):
        pl.when(sends)(pltpu.make_async_copy(landed, landed, send_h.at[0, i, 0]).wait)
    move_rows(first, part, shift, tab_ref)
    end_edges(1)

    def last_columns(j, carry):
        g = lax.rem(y + j, 4)
        pl.when(lower)(lambda: west_copy_1(g).wait_recv())
        pl.when(upper)(lambda: east_copy_1(g).wait_recv())
        move_columns(g, part, second, west.at[1], east.at[1], edge_in.at[1], rows_ref, col_wet_ref, tab_ref)

        def send_back(i, carry):
            w = g * 32 + lax.rem(me + i, 32)
            pltpu.make_async_remote_copy(
                one(second, w), one(last, column), send_b, recv_b, device_id={"wide": w}, device_id_type=MESH
            ).start()
            return carry

        return lax.fori_loop((3 - j) // 3, 32, send_back, carry)

    lax.fori_loop(0, 4, last_columns, 0)
    pltpu.make_async_copy(one(second, me), one(last, column), recv_b).start()
    pltpu.make_async_copy(one(second, me), one(spare, 8), send_b).start()
    lax.fori_loop(0, 4, sent_columns, 0)
    pltpu.make_async_copy(wind_all.at[chunk(0, 8)], wind_all.at[chunk(0, 8)], send_w.at[0]).wait()
    pltpu.make_async_copy(others, others, send_w.at[1]).wait()
    pltpu.make_async_copy(last, last, recv_b).wait()
    pltpu.make_async_copy(second, second, send_b).wait()


def local(spectrum, wind_speed, wind_dir, wet_mask, row_block, plus_index, minus_index):
    dma, i32 = pltpu.SemaphoreType.DMA, jnp.int32
    vmem = lambda *shape, dtype=F32: pltpu.VMEM(shape, dtype)
    wide = NB + 128
    received = pl.pallas_call(
        kernel,
        out_shape=jax.ShapeDtypeStruct((128, NB), F32),
        in_specs=[pl.BlockSpec(memory_space=pl.ANY)] * 8,
        out_specs=pl.BlockSpec(memory_space=pltpu.VMEM),
        scratch_shapes=[
            vmem(NB, 128),
            vmem(1, 128),
            vmem(1, 128),
            vmem(128, 128, dtype=i32),
            vmem(1, 128, dtype=i32),
            vmem(TILES, 128, dtype=i32),
            vmem(TILES, 128, dtype=i32),
            vmem(16, NB),
            dma((8,)),
            vmem(2, NB, 128),
            vmem(128, NB),
            vmem(128, NB),
            vmem(128, NB),
            vmem(8, 256),
            vmem(128, 256),
            vmem(2, 128, HALF),
            vmem(2, 128, HALF),
            vmem(2, 16, NB),
            vmem(2, 16, NB),
            vmem(128, 128),
            vmem(128, 128),
            vmem(TILES, 256, 256, dtype=BF16),
            vmem(128, wide, dtype=BF16),
            vmem(2, 128, NB),
            vmem(128, wide, dtype=BF16),
            vmem(2, 128, NB),
            vmem(16, NB),
            vmem(8, 256),
            dma,
            dma((16,)),
            dma((2,)),
            dma((2,)),
            dma((2, 2, 4)),
            dma((2, 2, 4)),
            dma((2, 2)),
            dma((2, 2)),
            dma,
            dma,
        ],
        compiler_params=pltpu.CompilerParams(
            collective_id=0, has_side_effects=True, vmem_limit_bytes=60 * 2**20
        ),
    )(
        spectrum,
        wind_speed.reshape(1, 128),
        wind_dir.reshape(1, 128),
        wet_mask,
        row_block,
        plus_index.reshape(TILES, 128),
        minus_index.reshape(TILES, 128),
        jnp.asarray(bin_table()),
    )
    return pl.pallas_call(to_bins, out_shape=jax.ShapeDtypeStruct((NB, 128), F32))(received)


def solution(mesh):
    placed = (
        P(None, ("wide", "sub")),
        P(("wide", "sub")),
        P(("wide", "sub")),
        P("sub", None),
        P("sub", None),
        P(),
        P(),
    )
    return jax.shard_map(
        local, mesh=mesh, in_specs=placed, out_specs=P(None, ("wide", "sub")), check_vma=False
    )
```

```python
import functools
import math

import jax
import jax.numpy as jnp
import numpy as np
from jax import lax
from jax.experimental import pallas as pl
from jax.experimental.pallas import tpu as pltpu
from jax.sharding import PartitionSpec as P

ND = 36
NF = 32
NB = ND * NF
NW = 128
NS = 4
TILES = NB // 128
HALF = 5 * 128
SPLIT = 19 * NF

WIND_COEF = 0.03
NONLIN_COEF = 0.004
DISS_COEF = 0.02
PLUS_WEIGHT = 0.4096
MINUS_WEIGHT = 3.1605
BOTH_WEIGHT = 1.2945
COURANT_MAX = 0.68
MESH = pl.DeviceIdType.MESH
F32 = jnp.float32
BF16 = jnp.bfloat16

RATE, GROW_X, GROW_Y, GROW_0, DAMP, DELTA, KEEP, MOVE_UP, MOVE_DOWN, MOVE_Y = range(10)


def bin_table():
    new = np.arange(NB)
    k, l = (new % NF).astype(np.float32), (new // NF).astype(np.float32)
    angles = l * np.float32(2.0 * math.pi / ND)
    rate = np.float32(1.0) + np.float32(0.1) * k
    speed = np.float32(1.0) / rate
    cx = np.float32(COURANT_MAX) * speed * np.cos(angles)
    cy = np.float32(COURANT_MAX) * speed * np.sin(angles)
    table = np.zeros((16, NB), np.float32)
    table[RATE] = rate
    table[GROW_X] = WIND_COEF * rate * rate / 40.0 * np.cos(angles)
    table[GROW_Y] = WIND_COEF * rate * rate / 40.0 * np.sin(angles)
    table[GROW_0] = WIND_COEF * rate
    table[DAMP] = DISS_COEF * rate
    table[DELTA] = NONLIN_COEF * rate
    table[KEEP] = 1.0 - np.abs(cx) - np.abs(cy)
    table[MOVE_UP] = np.maximum(cx, 0.0)
    table[MOVE_DOWN] = np.maximum(-cx, 0.0)
    table[MOVE_Y] = np.abs(cy)
    assert (cy[:SPLIT] >= 0).all() and (cy[SPLIT:] <= 0).all()
    return table


def column_of(w, strip):
    w = lax.rem(w + 32 * lax.rem(strip, 2), NW)
    plane, z = w // 8, lax.rem(w, 8)
    z = z + (strip // 2) * (7 - 2 * z)
    y, x = plane // 4, lax.rem(plane, 4)
    turn = lax.rem(y, 2)
    p = y * 4 + x + turn * (3 - 2 * x)
    back = lax.rem(z, 2)
    return z * 16 + p + back * (15 - 2 * p)


def device_of(c, strip):
    z, q = c // 16, lax.rem(c, 16)
    back = lax.rem(z, 2)
    p = q + back * (15 - 2 * q)
    y, i = p // 4, lax.rem(p, 4)
    turn = lax.rem(y, 2)
    x = i + turn * (3 - 2 * i)
    z = z + (strip // 2) * (7 - 2 * z)
    return lax.rem((y * 4 + x) * 8 + z + 96 * lax.rem(strip, 2), NW)


def lanes(t, count=1):
    start = t * 128 if isinstance(t, int) else pl.multiple_of(t * 128, 128)
    return pl.ds(start, 128 * count)


def chunk(g, size=32):
    return pl.ds(pl.multiple_of(g * size, size), size)


def spread(row):
    return jnp.transpose(jnp.broadcast_to(row, (128, 128)))


def build_partners(up_ref, down_ref, column_ref, hot_ref):
    lane = lax.broadcasted_iota(jnp.int32, (128, 128), 1).astype(F32)
    for side, ref in enumerate((up_ref, down_ref)):
        index = ref[...].astype(F32)
        frequency = jnp.floor((index + 0.5) * (1.0 / ND))
        index = (index - ND * frequency) * NF + frequency
        index = jnp.transpose(jnp.concatenate([index, jnp.zeros((128 - TILES, 128), F32)], axis=0))
        for r in range(TILES):
            column_ref[side, r * 128 : r * 128 + 128, :] = jnp.broadcast_to(index[:, r : r + 1], (128, 128))
    for t in range(TILES):
        for side in range(2):
            tile = (t + side) % TILES
            index = [column_ref[side, pl.ds(4 * tile + i, NF, stride=ND), :] for i in range(4)]
            index = jnp.concatenate(index, axis=0) - 128.0 * t
            index = jnp.where(index < 0.0, index + NB, index)
            both = [(index == lane + 128.0 * half).astype(F32).astype(BF16) for half in range(2)]
            hot_ref[t, side * 128 : side * 128 + 128, :] = jnp.concatenate(both, axis=1)


def sources(field, wind_x, wind_y, wet, tab_ref, hot_ref, round_ref, pair_ref, delta_ref, add_ref):
    total = jnp.zeros((128, 128), F32)
    for t in range(TILES):
        f = field[:, lanes(t)]
        round_ref[:, lanes(t)] = f.astype(BF16)
        scaled = f * tab_ref[RATE : RATE + 1, lanes(t)]
        total = total + scaled * scaled
    round_ref[:, lanes(TILES)] = round_ref[:, lanes(0)]
    steep = jnp.sqrt(jnp.sum(total, axis=1, keepdims=True) * (1.0 / NB) + 1e-06)
    steep = jnp.broadcast_to(steep, (128, 128))

    def gather(t):
        both = lax.dot_general(
            round_ref[:, lanes(t, 2)], hot_ref[t], (((1,), (1,)), ((), ())), preferred_element_type=F32
        )
        pair_ref[0, :, lanes(t)] = both[:, :128]
        pair_ref[1, :, lanes((t + 1) % TILES)] = both[:, 128:]

    for t in range(TILES):
        gather(t)

    def combine(t):
        f = field[:, lanes(t)]
        plus, minus = pair_ref[0, :, lanes(t)], pair_ref[1, :, lanes(t)]
        row = lambda r: tab_ref[r : r + 1, lanes(t)]
        delta = (row(DELTA) * f) * (
            f * (PLUS_WEIGHT * plus + MINUS_WEIGHT * minus) - (2.0 * BOTH_WEIGHT) * plus * minus
        )
        delta_ref[:, lanes(t)] = delta.astype(BF16)
        growth = jnp.maximum(wind_x * row(GROW_X) + wind_y * row(GROW_Y) - row(GROW_0), 0.0)
        field[:, lanes(t)] = f + growth * f - (row(DAMP) * steep) * f - 2.0 * delta

    for t in range(TILES):
        combine(t)
    delta_ref[:, lanes(TILES)] = delta_ref[:, lanes(0)]

    def scatter(t):
        back = jnp.dot(delta_ref[:, lanes(t, 2)], hot_ref[t], preferred_element_type=F32)
        add_ref[0, :, lanes(t)] = back[:, :128]
        add_ref[1, :, lanes((t + 1) % TILES)] = back[:, 128:]

    for t in range(TILES):
        scatter(t)

    def finish(t):
        field[:, lanes(t)] = wet * (field[:, lanes(t)] + add_ref[0, :, lanes(t)] + add_ref[1, :, lanes(t)])

    for t in range(TILES):
        finish(t)


def move_rows(src, part, shift, tab_ref):
    for t in range(TILES):
        f = src[:, lanes(t)]
        high = f.astype(BF16)
        low = (f - high.astype(F32)).astype(BF16)
        moved = jnp.dot(shift, jnp.concatenate([high, low], axis=0), preferred_element_type=F32)
        row = lambda r: tab_ref[r : r + 1, lanes(t)]
        part[:, lanes(t)] = row(KEEP) * f + row(MOVE_UP) * moved[:128] + row(MOVE_DOWN) * moved[128:]


def move_columns(g, part, dst, west, east, edges, rows, wet, tab_ref):
    at = chunk(g)
    lane = lax.broadcasted_iota(jnp.int32, (32, 128), 1)
    top, bottom, here = rows[at, :] == 0.0, rows[at, :] == float(NW - 1), wet[at, :]
    for t in range(TILES):
        cols = slice(t * 128, t * 128 + 128)
        row = lambda r: tab_ref[r : r + 1, cols]
        if t < 4:
            near_y = west[at, cols]
        elif t > 4:
            near_y = east[at, (t - 4) * 128 : (t - 3) * 128]
        else:
            near_y = jnp.where(lane < SPLIT - 512, west[at, cols], east[at, 0:128])
        above = jnp.where(top, row(MOVE_UP) * edges[0:1, cols], 0.0)
        below = jnp.where(bottom, row(MOVE_DOWN) * edges[8:9, cols], 0.0)
        dst[at, cols] = here * (part[at, cols] + above + below + row(MOVE_Y) * near_y)


def to_bins(last, out):
    for t in range(TILES):
        block = jnp.transpose(last[:, t * 128 : t * 128 + 128])
        for i in range(4):
            out[pl.ds(4 * t + i, NF, stride=ND), :] = block[i * NF : (i + 1) * NF]


def kernel(
    spectrum_in,
    speed_in,
    direction_in,
    wet_in,
    order_in,
    up_in,
    down_in,
    tab_in,
    last,
    spectrum,
    speed,
    direction,
    wet_ref,
    order_ref,
    up_ref,
    down_ref,
    tab_ref,
    load,
    index_ref,
    first,
    second,
    part,
    wind_row,
    wind_all,
    west,
    east,
    edge_out,
    edge_in,
    rows_ref,
    col_wet_ref,
    hot,
    rounded,
    pair,
    delta,
    add,
    spare,
    spare_w,
    send_a,
    recv_a,
    send_w,
    recv_w,
    send_h,
    recv_h,
    send_e,
    recv_e,
    send_b,
    recv_b,
):
    me = lax.axis_index("wide")
    strip = lax.axis_index("sub")
    plane, z, y = me // 8, lax.rem(me, 8), me // 32
    column = column_of(me, strip)
    lower, upper = column > 0, column < NW - 1
    to_lower, to_upper = device_of(jnp.maximum(column - 1, 0), strip), device_of(jnp.minimum(column + 1, NW - 1), strip)
    to_above = device_of(column, jnp.maximum(strip - 1, 0))
    to_below = device_of(column, jnp.minimum(strip + 1, NS - 1))
    has_above, has_below = strip > 0, strip < NS - 1
    one = lambda ref, i: ref.at[pl.ds(i, 1)]

    for k in range(2):
        for is_there, blank in (
            (lower, west.at[k]),
            (upper, east.at[k]),
            (has_above, edge_in.at[k, 0:8]),
            (has_below, edge_in.at[k, 8:16]),
        ):

            @pl.when(jnp.logical_not(is_there))
            def _(blank=blank):
                blank[...] = jnp.zeros(blank.shape, F32)

    barrier = pltpu.get_barrier_semaphore()
    line_peer = lambda i: plane * 8 + lax.rem(z + i, 8)
    plane_peer = lambda i: lax.rem(plane + i, 16) * 8 + z

    def greet(peer, sem):
        def signal(i, carry):
            pl.semaphore_signal(sem, inc=1, device_id={"wide": peer(i)}, device_id_type=MESH)
            return carry

        return signal

    lax.fori_loop(1, NW, greet(lambda i: lax.rem(me + i, NW), barrier), 0)

    @pl.when(has_above)
    def _():
        pl.semaphore_signal(barrier, inc=1, device_id={"wide": to_above, "sub": strip - 1}, device_id_type=MESH)

    @pl.when(has_below)
    def _():
        pl.semaphore_signal(barrier, inc=1, device_id={"wide": to_below, "sub": strip + 1}, device_id_type=MESH)

    inputs = (
        (up_in, up_ref),
        (down_in, down_ref),
        (speed_in, speed),
        (direction_in, direction),
        (wet_in, wet_ref),
        (order_in, order_ref),
        (tab_in, tab_ref),
        (spectrum_in, spectrum),
    )
    inputs = [pltpu.make_async_copy(src, dst, load.at[i]) for i, (src, dst) in enumerate(inputs)]
    for copy in inputs:
        copy.start()
    for copy in inputs[:-1]:
        copy.wait()

    row_ids = lax.broadcasted_iota(jnp.int32, (128, 128), 0).astype(F32)
    lane_ids = lax.broadcasted_iota(jnp.int32, (128, 128), 1).astype(F32)
    ones = jnp.ones((128, 128), BF16)
    order = order_ref[...].astype(F32)
    rows = spread(order)
    rows_ref[...] = rows
    wet_grid = wet_ref[...].astype(F32)
    mine = jnp.sum(jnp.where(lane_ids == me.astype(F32), order, 0.0), axis=1, keepdims=True)
    own_wet = jnp.where(row_ids == mine, wet_grid, 0.0).astype(BF16)
    own_wet = lax.dot_general(own_wet, ones, (((0,), (0,)), ((), ())), preferred_element_type=F32)
    col_wet = jnp.where(lane_ids == column.astype(F32), wet_grid, 0.0).astype(BF16)
    col_wet = jnp.dot(col_wet, ones, preferred_element_type=F32).astype(BF16)
    pick = (lane_ids == rows).astype(F32).astype(BF16)
    col_wet_ref[...] = jnp.dot(pick, col_wet, preferred_element_type=F32)
    above_hot = (order == rows - 1.0).astype(F32)
    below_hot = (order == rows + 1.0).astype(F32)
    shift = jnp.concatenate([above_hot, below_hot], axis=0)
    shift = jnp.concatenate([shift, shift], axis=1).astype(BF16)

    wind_x = speed[...] * jnp.cos(direction[...])
    wind_y = speed[...] * jnp.sin(direction[...])
    wind_row[0:1, 0:128] = wind_x
    wind_row[0:1, 128:256] = wind_y
    build_partners(up_ref, down_ref, index_ref, hot)
    inputs[-1].wait()
    for t in range(TILES):
        block = jnp.concatenate([spectrum[pl.ds(4 * t + i, NF, stride=ND), :] for i in range(4)], axis=0)
        first[:, t * 128 : t * 128 + 128] = jnp.transpose(block)
    sources(first, spread(wind_x), spread(wind_y), own_wet, tab_ref, hot, rounded, pair, delta, add)

    beside = has_above.astype(jnp.int32) + has_below.astype(jnp.int32)
    pl.semaphore_wait(barrier, NW - 1 + beside)

    pltpu.make_async_copy(one(wind_row, 0), one(wind_all, me), recv_w.at[0]).start()
    pltpu.make_async_copy(one(wind_row, 0), one(spare_w, 0), send_w.at[0]).start()

    def send_line(i, carry):
        pltpu.make_async_remote_copy(
            one(wind_row, 0),
            one(wind_all, me),
            send_w.at[0],
            recv_w.at[0],
            device_id={"wide": line_peer(i)},
            device_id_type=MESH,
        ).start()
        return carry

    lax.fori_loop(1, 8, send_line, 0)

    pltpu.make_async_copy(one(first, column), one(second, me), recv_a.at[plane]).start()
    pltpu.make_async_copy(one(first, column), one(spare, 0), send_a).start()

    def send_out(i, carry):
        w = lax.rem(me + i, NW)
        pltpu.make_async_remote_copy(
            one(first, column_of(w, strip)),
            one(second, me),
            send_a,
            recv_a.at[plane],
            device_id={"wide": w},
            device_id_type=MESH,
        ).start()
        return carry

    lax.fori_loop(1, NW, send_out, 0)

    wind_line = wind_all.at[chunk(plane, 8)]
    pltpu.make_async_copy(wind_line, wind_line, recv_w.at[0]).wait()

    def send_plane(i, carry):
        pltpu.make_async_remote_copy(
            wind_line,
            wind_line,
            send_w.at[1],
            recv_w.at[1],
            device_id={"wide": plane_peer(i)},
            device_id_type=MESH,
        ).start()
        return carry

    lax.fori_loop(1, 16, send_plane, 0)

    def side_copies(k, field):
        def west_copy(g):
            return pltpu.make_async_remote_copy(
                field.at[chunk(g), 0:HALF],
                west.at[k, chunk(g)],
                send_h.at[k, 0, g],
                recv_h.at[k, 0, g],
                device_id={"wide": to_upper},
                device_id_type=MESH,
            )

        def east_copy(g):
            return pltpu.make_async_remote_copy(
                field.at[chunk(g), NB - HALF : NB],
                east.at[k, chunk(g)],
                send_h.at[k, 1, g],
                recv_h.at[k, 1, g],
                device_id={"wide": to_lower},
                device_id_type=MESH,
            )

        return west_copy, east_copy

    def edge_copies(k):
        return [
            (
                sends,
                gets,
                pltpu.make_async_remote_copy(
                    edge_out.at[k, pl.ds(8 * i, 1)],
                    edge_in.at[k, pl.ds(8 * i, 1)],
                    send_e.at[k, i],
                    recv_e.at[k, i],
                    device_id=to,
                    device_id_type=MESH,
                ),
            )
            for i, sends, gets, to in (
                (0, has_below, has_above, {"wide": to_below, "sub": jnp.minimum(strip + 1, NS - 1)}),
                (1, has_above, has_below, {"wide": to_above, "sub": jnp.maximum(strip - 1, 0)}),
            )
        ]

    def start_edges(k, field):
        rows = rows_ref[...]

        for t in range(TILES):
            f = field[:, lanes(t)]
            edge_out[k, 0:1, lanes(t)] = jnp.sum(jnp.where(rows == float(NW - 1), f, 0.0), axis=0, keepdims=True)
            edge_out[k, 8:9, lanes(t)] = jnp.sum(jnp.where(rows == 0.0, f, 0.0), axis=0, keepdims=True)

        for sends, gets, copy in edge_copies(k):
            pl.when(sends)(copy.start)

    def end_edges(k):
        for sends, gets, copy in edge_copies(k):
            pl.when(gets)(copy.wait_recv)
            pl.when(sends)(copy.wait_send)

    west_copy_1, east_copy_1 = side_copies(1, first)

    first_sides = (
        (
            upper,
            lower,
            lambda g: pltpu.make_async_remote_copy(
                second.at[chunk(g, 8), 0:HALF],
                west.at[0, chunk(g, 8)],
                send_h.at[0, 0, 0],
                recv_h.at[0, 0, 0],
                device_id={"wide": to_upper},
                device_id_type=MESH,
            ),
            west.at[0],
        ),
        (
            lower,
            upper,
            lambda g: pltpu.make_async_remote_copy(
                second.at[chunk(g, 8), NB - HALF : NB],
                east.at[0, chunk(g, 8)],
                send_h.at[0, 1, 0],
                recv_h.at[0, 1, 0],
                device_id={"wide": to_lower},
                device_id_type=MESH,
            ),
            east.at[0],
        ),
    )

    def pass_on(j, carry):
        g = lax.rem(plane + 15 - j, 16)
        pltpu.make_async_copy(second.at[chunk(g, 8)], second.at[chunk(g, 8)], recv_a.at[g]).wait()
        for sends, gets, copy, landed in first_sides:
            pl.when(jnp.logical_and(sends, j < 15))(lambda copy=copy: copy(g).start())
        return carry

    lax.fori_loop(0, 16, pass_on, 0)
    start_edges(0, second)
    for sends, gets, copy, landed in first_sides:
        pl.when(sends)(lambda copy=copy: copy(plane).start())
    move_rows(second, part, shift, tab_ref)
    end_edges(0)

    for i, (sends, gets, copy, landed) in enumerate(first_sides):
        pl.when(gets)(pltpu.make_async_copy(landed, landed, recv_h.at[0, i, 0]).wait)

    pltpu.make_async_copy(first, first, send_a).wait()

    def first_columns(g, carry):
        move_columns(g, part, first, west.at[0], east.at[0], edge_in.at[0], rows_ref, col_wet_ref, tab_ref)
        return carry

    lax.fori_loop(0, 4, first_columns, 0)

    def sent_columns(g, carry):
        pl.when(upper)(lambda: west_copy_1(g).wait_send())
        pl.when(lower)(lambda: east_copy_1(g).wait_send())
        return carry

    others = wind_all.at[pl.ds(0, 120)]
    pltpu.make_async_copy(others, others, recv_w.at[1]).wait()
    here = lane_ids == column.astype(F32)
    wind_x, wind_y = (
        jnp.broadcast_to(
            jnp.sum(jnp.where(here, wind_all[:, i * 128 : i * 128 + 128], 0.0), axis=1, keepdims=True), (128, 128)
        )
        for i in range(2)
    )
    sources(first, wind_x, wind_y, col_wet_ref[...], tab_ref, hot, rounded, pair, delta, add)
    start_edges(1, first)
    y_upper, y_lower = to_upper // 32, to_lower // 32

    def start_columns(j, carry):
        pl.when(upper)(lambda: west_copy_1(lax.rem(y_upper + j, 4)).start())
        pl.when(lower)(lambda: east_copy_1(lax.rem(y_lower + j, 4)).start())
        return carry

    lax.fori_loop(0, 4, start_columns, 0)
    move_rows(first, part, shift, tab_ref)
    end_edges(1)
    for i, (sends, gets, copy, landed) in enumerate(first_sides):
        pl.when(sends)(pltpu.make_async_copy(landed, landed, send_h.at[0, i, 0]).wait)

    def last_columns(j, carry):
        g = lax.rem(y + j, 4)
        pl.when(lower)(lambda: west_copy_1(g).wait_recv())
        pl.when(upper)(lambda: east_copy_1(g).wait_recv())
        move_columns(g, part, second, west.at[1], east.at[1], edge_in.at[1], rows_ref, col_wet_ref, tab_ref)

        def send_back(i, carry):
            w = g * 32 + lax.rem(me + i, 32)
            pltpu.make_async_remote_copy(
                one(second, w), one(last, column), send_b, recv_b, device_id={"wide": w}, device_id_type=MESH
            ).start()
            return carry

        return lax.fori_loop((3 - j) // 3, 32, send_back, carry)

    lax.fori_loop(0, 4, last_columns, 0)
    pltpu.make_async_copy(one(second, me), one(last, column), recv_b).start()
    pltpu.make_async_copy(one(second, me), one(spare, 8), send_b).start()
    lax.fori_loop(0, 4, sent_columns, 0)
    pltpu.make_async_copy(wind_all.at[chunk(0, 8)], wind_all.at[chunk(0, 8)], send_w.at[0]).wait()
    pltpu.make_async_copy(others, others, send_w.at[1]).wait()
    pltpu.make_async_copy(last, last, recv_b).wait()
    pltpu.make_async_copy(second, second, send_b).wait()


def local(spectrum, wind_speed, wind_dir, wet_mask, row_block, plus_index, minus_index):
    dma, i32 = pltpu.SemaphoreType.DMA, jnp.int32
    vmem = lambda *shape, dtype=F32: pltpu.VMEM(shape, dtype)
    wide = NB + 128
    received = pl.pallas_call(
        kernel,
        out_shape=jax.ShapeDtypeStruct((128, NB), F32),
        in_specs=[pl.BlockSpec(memory_space=pl.ANY)] * 8,
        out_specs=pl.BlockSpec(memory_space=pltpu.VMEM),
        scratch_shapes=[
            vmem(NB, 128),
            vmem(1, 128),
            vmem(1, 128),
            vmem(128, 128, dtype=i32),
            vmem(1, 128, dtype=i32),
            vmem(TILES, 128, dtype=i32),
            vmem(TILES, 128, dtype=i32),
            vmem(16, NB),
            dma((8,)),
            vmem(2, NB, 128),
            vmem(128, NB),
            vmem(128, NB),
            vmem(128, NB),
            vmem(8, 256),
            vmem(128, 256),
            vmem(2, 128, HALF),
            vmem(2, 128, HALF),
            vmem(2, 16, NB),
            vmem(2, 16, NB),
            vmem(128, 128),
            vmem(128, 128),
            vmem(TILES, 256, 256, dtype=BF16),
            vmem(128, wide, dtype=BF16),
            vmem(2, 128, NB),
            vmem(128, wide, dtype=BF16),
            vmem(2, 128, NB),
            vmem(16, NB),
            vmem(8, 256),
            dma,
            dma((16,)),
            dma((2,)),
            dma((2,)),
            dma((2, 2, 4)),
            dma((2, 2, 4)),
            dma((2, 2)),
            dma((2, 2)),
            dma,
            dma,
        ],
        compiler_params=pltpu.CompilerParams(
            collective_id=0, has_side_effects=True, vmem_limit_bytes=60 * 2**20
        ),
    )(
        spectrum,
        wind_speed.reshape(1, 128),
        wind_dir.reshape(1, 128),
        wet_mask,
        row_block,
        plus_index.reshape(TILES, 128),
        minus_index.reshape(TILES, 128),
        jnp.asarray(bin_table()),
    )
    return pl.pallas_call(to_bins, out_shape=jax.ShapeDtypeStruct((NB, 128), F32))(received)


def solution(mesh):
    placed = (
        P(None, ("wide", "sub")),
        P(("wide", "sub")),
        P(("wide", "sub")),
        P("sub", None),
        P("sub", None),
        P(),
        P(),
    )
    return jax.shard_map(
        local, mesh=mesh, in_specs=placed, out_specs=P(None, ("wide", "sub")), check_vma=False
    )
```
